32 devices in a mesh: grp: 2 (over y), chan: 4 (over z), tblk: 4 (over x, core).
Axes of the slice: x: 2, y: 2, z: 4, core: 2. Of those that a mesh axis runs over, the one named last changes fastest.
Arguments:
- coarse_volts: bfloat16 [2048, 2, 2, 3072], P('chan', None, 'grp', 'tblk'), parts along dimension 2, may hold values from -6 to 6
- lead_in: bfloat16 [2048, 2, 2, 48], P('chan', None, 'grp'), parts along dimension 2, may hold values from -6 to 6
- slot_of_input: int32 [2048], replicated, may hold values from 0 to 2047, each once
Outputs:
- fine_voltages: bfloat16 [8, 192, 4096], P(('grp', 'chan'), 'tblk'), parts along dimension 0
- visibilities: bfloat16 [8, 4096, 4096], P(('grp', 'chan'), 'tblk'), parts along dimension 0
The draws below stay inside these ranges and needn't reach their ends.
There are 2 independent parts, one for each index of `grp`. The reference program is written for one: setup_inputs(seed, part) draws one part's arguments, and reference() takes and returns one part's arrays. A program takes and returns all parts, laid end to end along the dimension named above; an argument that names none is the same for every part. Nothing has to cross between parts.
Inputs may be any that keep to these rules, and one draw needn't show every extreme that they name: `slot_of_input`: each slot holds exactly one input.
All inputs are finite; a program needn't handle non-finite values.
Results may differ from the reference program's by a relative error of at most 0.0057.
Values may be sent and summed in bfloat16 or wider, within the bound.
No kernel may reach another device: no remote copies, remote signals or barrier semaphores. Data moves between devices by JAX's collectives and lax.ppermute only.
A program may use at most 64 MiB of HBM per device.

```python
import math
import jax
import jax.numpy as jnp
from jax import lax

INPUTS = 2048
UPCHAN = 16
TAPS = 4
LEAD = 48
CHANNELS = 4
COARSE = 1
TIME = 192
SAMPLES = 3072


def block_scale(own_key, shape, shards, least, largest):
    gain, own = 1.0, jax.random.fold_in(own_key, 6)
    for axis_at, blocks in shards:
        steps = jnp.exp(jax.random.uniform(jax.random.fold_in(own, axis_at), (blocks,), jnp.float32, least / len(shards), largest / len(shards)))
        gain = gain * jnp.repeat(steps, shape[axis_at] // blocks).reshape([-1 if axis == axis_at else 1 for axis in range(len(shape))])
    return gain


def bell_draw(key, dims, width, bound, split=(), kind=jnp.bfloat16):
    values = jax.random.normal(key, dims, jnp.float32) * width
    if len(split) > 0:
        values = block_scale(key, dims, split, -0.22, 0.18) * values
    return jnp.clip(values, min=-bound, max=bound).astype(kind)


def setup_inputs(seed: int = 0, part: int = 0) -> dict:
    key_of = jax.random.split(jax.random.key(seed), 4)
    own_keys = jax.random.split(jax.random.fold_in(key_of[3], part), 4)
    coarse_volts = bell_draw(own_keys[0], (INPUTS, 2, COARSE, SAMPLES), 1.0, 6.0, ((0, 4), (3, 4)))
    lead_in = bell_draw(own_keys[1], (INPUTS, 2, COARSE, LEAD), 1.0, 6.0, ((0, 4),))
    slot_of_input = jax.random.permutation(key_of[2], INPUTS).astype(jnp.int32)
    return {"coarse_volts": coarse_volts, "lead_in": lead_in, "slot_of_input": slot_of_input}


def filter_table():
    length = TAPS * UPCHAN
    taps = jnp.arange(length, dtype=jnp.int32)
    place = taps.astype(jnp.float32)
    center = (length - 1) / 2.0
    window = jnp.sinc((place - center) / UPCHAN) * (0.5 - 0.5 * jnp.cos(2.0 * math.pi * (place + 0.5) / length))
    window = window / jnp.sqrt(jnp.sum(window * window))
    bins = jnp.arange(UPCHAN, dtype=jnp.int32)
    turns = (taps % UPCHAN)[:, None] * bins[None, :] % UPCHAN
    phase = 2.0 * math.pi * turns.astype(jnp.float32) / UPCHAN
    cosine = window[:, None] * jnp.cos(phase)
    sine = window[:, None] * jnp.sin(phase)
    from_real = jnp.stack([cosine, -sine], axis=1)
    from_imag = jnp.stack([sine, cosine], axis=1)
    table = jnp.stack([from_real, from_imag], axis=0)
    return table.reshape(2, TAPS, UPCHAN, 2, UPCHAN)

def channelize(volts, history):
    extended = jnp.concatenate([history, volts], axis=3).astype(jnp.float32)
    inputs, parts, coarse, length = extended.shape
    count = length // UPCHAN
    frames = count - TAPS + 1
    blocks = extended.reshape(inputs, parts, coarse, count, UPCHAN)
    table = filter_table()
    total = jnp.zeros((coarse, UPCHAN, frames, 2, inputs), jnp.float32)
    for step in range(TAPS):
        total = total + jnp.einsum('ipctr,prok->cktoi', blocks[:, :, :, step:step + frames, :], table[:, step], precision=lax.Precision.HIGHEST)
    return total.reshape(coarse * UPCHAN, frames, 2, inputs)

def reference(coarse_volts, lead_in, slot_of_input):
    spectrum = channelize(coarse_volts, lead_in)[:CHANNELS].astype(jnp.bfloat16)
    ordered = jnp.take(spectrum, slot_of_input, axis=3).reshape(CHANNELS, TIME, 2 * INPUTS)

    def one_channel(series):
        values = series.astype(jnp.float32)
        gram = jnp.dot(values.T, values, precision=lax.Precision.HIGHEST)
        return (gram / TIME).astype(jnp.bfloat16)
    visibilities = lax.map(one_channel, ordered)
    return (ordered, visibilities)
```

```python
import functools
import math

import jax
import jax.numpy as jnp
import ml_dtypes
import numpy as np
from jax import lax
from jax.experimental import pallas as pl
from jax.experimental.pallas import tpu as pltpu
from jax.sharding import PartitionSpec as P

UPCHAN = 16
TAPS = 4
GROUP = 16
PAD = 128
MIB = 1 << 20
VMEM = pl.BlockSpec(memory_space=pltpu.VMEM)
HBM = pl.BlockSpec(memory_space=pltpu.HBM)


def shifted(value, axis, steps):
    count = lax.axis_size(axis)
    leading, last = (max(0, -steps), min(count, count - steps))
    return lax.ppermute(value, axis, [(source, source + steps) for source in range(leading, last)])


def swapped(value, axis, distance):
    count = lax.axis_size(axis)
    return lax.ppermute(value, axis, [(source, source ^ distance) for source in range(count)])


def filter_table(bins):
    length = TAPS * UPCHAN
    taps = np.arange(length)
    center = (length - 1) / 2.0
    window = np.sinc((taps - center) / UPCHAN) * (0.5 - 0.5 * np.cos(2.0 * math.pi * (taps + 0.5) / length))
    window = window / np.sqrt(np.sum(window * window))
    phase = 2.0 * math.pi * ((taps % UPCHAN)[None, :] * np.arange(bins)[:, None] % UPCHAN) / UPCHAN
    cosine, sine = window * np.cos(phase), window * np.sin(phase)
    real = np.stack([cosine, sine], axis=-1)
    imag = np.stack([-sine, cosine], axis=-1)
    return np.stack([real, imag], axis=1).astype(np.float32)


def halves(table):
    high = table.astype(ml_dtypes.bfloat16)
    low = (table - high.astype(np.float32)).astype(ml_dtypes.bfloat16)
    return high, low


def group_table(bins, steps, offset, width, frames):
    taps = filter_table(bins)
    table = np.zeros((bins, 2, frames, 2, width), np.float32)
    for frame in range(steps):
        for tap in range(TAPS * UPCHAN):
            sample = offset + UPCHAN * frame + tap
            if 0 <= sample < width:
                table[:, :, frame, :, sample] = taps[:, :, tap, :]
    high, low = halves(table.reshape(bins, 2 * frames, 2, width))
    return np.stack([high, low], axis=1)


def dot_samples(table, samples):
    return lax.dot_general(table, samples, (((1,), (1,)), ((), ())), preferred_element_type=jnp.float32)


def history_kernel(bins_per_coarse, volts_hbm, table_hbm, tail_ref, samples_ref, table_ref, pairs_ref, sems):
    width = volts_hbm.shape[3]
    rows = table_hbm.shape[2]
    copies = [
        pltpu.make_async_copy(volts_hbm.at[:, :, :, pl.ds(width - PAD, PAD)], samples_ref, sems.at[0]),
        pltpu.make_async_copy(table_hbm, table_ref, sems.at[1]),
    ]
    for copy in copies:
        copy.start()
    for copy in copies:
        copy.wait()
    at = 0
    for coarse, bins in enumerate(bins_per_coarse):
        total = 0.0
        for part, samples in enumerate(parts_of(samples_ref, pairs_ref, coarse, 0)):
            for half in range(2):
                table = table_ref[:bins, half, :, part * PAD : (part + 1) * PAD].reshape(bins * rows, PAD)
                total = total + dot_samples(table, samples)
        tail_ref[at : at + bins * rows, :] = total
        at += bins * rows


def parts_of(samples_ref, pairs_ref, coarse, lane):
    slots = samples_ref.shape[0]
    pairs = samples_ref[:, coarse, :, lane : lane + PAD].reshape(2 * slots, PAD)
    place = lane * 2 * slots // PAD
    pairs_ref[place : place + 2 * slots, :] = pairs.astype(jnp.float32)
    return [pairs_ref[pl.ds(place + part, slots, stride=2), :].astype(jnp.bfloat16) for part in range(2)]


def channel_kernel(plan, volts_ref, lead_ref, table_ref, lead_table_ref, *refs):
    spectrum_refs, early_ref, pairs_ref = refs[:-2], refs[-2], refs[-1]
    slots, _, _, width = volts_ref.shape
    lead_width = lead_ref.shape[2]
    frames = width // UPCHAN
    groups = frames // GROUP
    span = PAD + GROUP * UPCHAN
    first = lax.axis_index("tblk") == 0
    me = lax.axis_index("chan")
    for coarse, members in plan:
        bins = [lax.bitwise_xor(me, distance) if relative else distance for relative, distance, _ in members]
        count = len(bins)
        table = [table_ref[pl.ds(k, 1), half] for half in range(2) for k in bins]
        table = jnp.concatenate(table, axis=0).reshape(2 * count * 2 * GROUP, 2 * span)
        lead_table = [lead_table_ref[pl.ds(k, 1), half] for half in range(2) for k in bins]
        lead_table = jnp.concatenate(lead_table, axis=0).reshape(2 * count * 8, 2 * lead_width)
        head = 0.0
        for part in range(2):
            lead = lead_ref[part, coarse, :, :]
            head = head + jnp.dot(
                lead_table[:, part * lead_width : (part + 1) * lead_width], lead, preferred_element_type=jnp.float32
            )
        head = jnp.where(first, head[: count * 8] + head[count * 8 :], 0.0).reshape(count, 2, 4, slots)
        samples = [parts_of(volts_ref, pairs_ref, coarse, lane) for lane in range(0, width, PAD)]
        for group in range(groups):
            total = 0.0
            for lane in range(span // PAD):
                at = group * GROUP * UPCHAN // PAD - 1 + lane
                if at < 0:
                    continue
                for part in range(2):
                    columns = part * span + lane * PAD
                    total = total + dot_samples(table[:, columns : columns + PAD], samples[at][part])
            total = total.reshape(2, count, 2, GROUP, slots)
            total = total[0] + total[1]
            if group == 0:
                opening = total[:, :, :4, :] + head
                row = (coarse * UPCHAN) * 8
                early_ref[row : row + count * 8, :] = opening.reshape(count * 8, slots)
            for at, (_, _, (out, index)) in enumerate(members):
                for part in range(2):
                    row = part * frames + group * GROUP
                    spectrum_refs[out][index, row : row + GROUP, :] = total[at, part].astype(jnp.bfloat16)


def early_kernel(plan, early_ref, history_ref, *refs):
    spectra_in, spectra_out = refs[: len(refs) // 2], refs[len(refs) // 2 :]
    me = lax.axis_index("chan")
    for coarse, members in plan:
        for at, (relative, distance, (out, index)) in enumerate(members):
            frames = spectra_in[out].shape[1] // 2
            bin_at = (lax.bitwise_xor(me, distance) if relative else distance) + coarse * UPCHAN
            row = (coarse * UPCHAN + at) * 8
            total = early_ref[row : row + 8, :] + history_ref[pl.ds(pl.multiple_of(bin_at * 8, 8), 8), :]
            for part in range(2):
                opening = total if part == 0 else pltpu.roll(total, 4, 0)
                opening = jnp.concatenate([opening, opening], axis=0)
                old = spectra_in[out][index, part * frames : part * frames + GROUP, :].astype(jnp.float32)
                row = lax.broadcasted_iota(jnp.int32, old.shape, 0)
                new = jnp.where(row < 4, opening, old).astype(jnp.bfloat16)
                spectra_out[out][index, part * frames : part * frames + GROUP, :] = new


def choice_kernel(relative, source, slots, slot_ref, choice_ref):
    owner = lax.bitwise_xor(lax.axis_index("chan"), source) if relative else source
    for row in range(0, choice_ref.shape[0], 64):
        rows = min(64, choice_ref.shape[0] - row)
        place = lax.broadcasted_iota(jnp.int32, (rows, slot_ref.shape[1]), 0) + (owner * slots + row)
        choice_ref[row : row + rows, :] = (place == slot_ref[...]).astype(jnp.bfloat16)


def order_kernel(places, fresh, choice_ref, *refs):
    pieces, old_ref, new_ref = refs[: len(places)], refs[-2], refs[-1]
    put_in_order(places, fresh, choice_ref, pieces, old_ref, new_ref)


def put_in_order(places, fresh, choice_ref, pieces, old_ref, new_ref):
    rows = pieces[0].shape[0]
    frames = rows // 2
    inputs = choice_ref.shape[1]
    stacked = jnp.concatenate([piece[...] for piece in pieces], axis=0)
    for column in range(0, inputs, 256):
        total = jnp.dot(stacked, choice_ref[:, column : column + 256], preferred_element_type=jnp.float32)
        total = total.astype(jnp.bfloat16)
        for at, place in enumerate(places):
            for part in range(2):
                value = total[at * rows + part * frames : at * rows + (part + 1) * frames]
                to = (slice(place * frames, (place + 1) * frames), slice(part * inputs + column, part * inputs + column + 256))
                new_ref[to] = value if fresh else old_ref[to] + value


def gram_kernel(blocks, relative, places, choice_ref, *refs):
    pieces, old_ref = refs[: len(places)], refs[len(places)]
    fine_hbm, gram_hbm, ordered, tile, result, sems = refs[len(places) + 1 :]
    frames = ordered.shape[0] // blocks
    width = tile.shape[0]
    own = 0 if relative else pl.multiple_of(lax.axis_index("tblk") * frames, frames)
    if places:
        inside = [place for place in range(blocks) if place not in places]
        for place in inside:
            ordered[place * frames : (place + 1) * frames, :] = old_ref[place * frames : (place + 1) * frames, :]
        put_in_order(places, False, choice_ref, pieces, old_ref, ordered)
    else:
        ordered[...] = old_ref[...]
    copies = [pltpu.make_async_copy(ordered.at[pl.ds(own, frames), :], fine_hbm, sems.at[0])]
    copies[0].start()
    place = pl.multiple_of(lax.axis_index("tblk") * width, width)
    tile[...] = ordered[:, pl.ds(place, width)].T
    chunk = width // 8
    for at in range(8):
        rows = slice(at * chunk, (at + 1) * chunk)
        gram = jnp.dot(tile[rows, :], ordered[...], preferred_element_type=jnp.float32)
        result[rows, :] = (gram * (1.0 / ordered.shape[0])).astype(jnp.bfloat16)
        copy = pltpu.make_async_copy(
            result.at[pl.ds(at * chunk, chunk), :], gram_hbm.at[pl.ds(at * chunk, chunk), :], sems.at[at + 1]
        )
        copy.start()
        copies.append(copy)
    for copy in copies:
        copy.wait()


def call(kernel, shapes, *operands, name, limit, spaces=VMEM, outs=VMEM, **options):
    spaces = spaces if isinstance(spaces, list) else [spaces] * len(operands)
    several = isinstance(shapes, list)
    return pl.pallas_call(
        kernel,
        in_specs=spaces,
        out_specs=[outs] * len(shapes) if several else outs,
        out_shape=shapes,
        compiler_params=pltpu.CompilerParams(vmem_limit_bytes=limit * MIB),
        name=name,
        **options,
    )(*operands)


def local(coarse_volts, lead_in, slot_of_input):
    slots, _, coarse, width = coarse_volts.shape
    lead_width = lead_in.shape[3]
    chans, blocks = lax.axis_size("chan"), lax.axis_size("tblk")
    frames = width // UPCHAN
    inputs = slot_of_input.shape[0]
    relative = coarse == 1 and chans == 4 and blocks == 4
    volts = coarse_volts.transpose(0, 2, 1, 3)
    lead = lead_in.transpose(1, 2, 3, 0)
    order = slot_of_input.reshape(1, inputs)

    per_coarse = [max(0, min(UPCHAN, chans - c * UPCHAN)) for c in range(coarse)]
    bins = max(per_coarse)
    span = PAD + GROUP * UPCHAN
    main = group_table(bins, GROUP, PAD - lead_width, span, GROUP)
    tail = group_table(bins, TAPS - 1, PAD - lead_width, PAD, 4)
    head = group_table(bins, TAPS - 1, 0, lead_width, 4)
    main, tail, head = (jnp.asarray(t.reshape(t.shape[:3] + (-1,))) for t in (main, tail, head))
    shape = jax.ShapeDtypeStruct

    opening = call(
        functools.partial(history_kernel, per_coarse),
        shape((chans * 8, slots), jnp.float32),
        volts,
        tail,
        name="history",
        limit=4,
        spaces=HBM,
        scratch_shapes=[
            pltpu.VMEM((slots, coarse, 2, PAD), jnp.bfloat16),
            pltpu.VMEM(tail.shape, jnp.bfloat16),
            pltpu.VMEM((2 * slots, PAD), jnp.float32),
            pltpu.SemaphoreType.DMA((2,)),
        ],
    )
    history = shifted(opening, "tblk", 1)

    if relative:
        plan = [(0, [(True, distance, (distance, 0)) for distance in range(chans)])]
        shapes = [shape((1, 2 * frames, slots), jnp.bfloat16)] * chans
    else:
        plan = [
            (c, [(False, k, (0, c * UPCHAN + k)) for k in range(count)]) for c, count in enumerate(per_coarse) if count
        ]
        shapes = [shape((chans, 2 * frames, slots), jnp.bfloat16)]
    *spectra, early = call(
        functools.partial(channel_kernel, plan),
        shapes + [shape((chans * 8, slots), jnp.float32)],
        volts,
        lead,
        main,
        head,
        name="channelize",
        limit=14,
        scratch_shapes=[pltpu.VMEM((2 * slots * width // PAD, PAD), jnp.float32)],
    )
    spectra = call(
        functools.partial(early_kernel, plan),
        shapes,
        early,
        history,
        *spectra,
        name="early",
        limit=2,
        input_output_aliases={2 + at: at for at in range(len(shapes))},
    )

    if relative:
        spectra = [s[0] for s in spectra]
        near = [spectra[0]] + [swapped(spectra[d], "chan", d) for d in (1, 2, 3)]
        pieces = []
        for piece in near:
            far = swapped(piece, "tblk", 2)
            pieces.append([piece, swapped(piece, "tblk", 1), far, swapped(far, "tblk", 1)])
    else:
        owned = lax.all_to_all(spectra[0], "chan", split_axis=0, concat_axis=2, tiled=True)[0]
        all_time = lax.all_gather(owned, "tblk", axis=0)
        pieces = [[all_time[b] for b in range(blocks)]]
        slots = inputs

    choices = [
        call(
            functools.partial(choice_kernel, relative, source, slots),
            shape((slots, inputs), jnp.bfloat16),
            order,
            name="choice",
            limit=2 if relative else 10,
        )
        for source in range(len(pieces))
    ]
    ordered_shape = shape((blocks * frames, 2 * inputs), jnp.bfloat16)
    ordered = jnp.zeros(ordered_shape.shape, ordered_shape.dtype)
    if relative:
        for source in range(3):
            ordered = call(
                functools.partial(order_kernel, list(range(blocks)), source == 0),
                ordered_shape,
                choices[source],
                *pieces[source],
                ordered,
                name="order",
                limit=6,
                input_output_aliases={1 + blocks: 0},
            )
        ordered = call(
            functools.partial(order_kernel, [0, 1], False),
            ordered_shape,
            choices[3],
            *pieces[3][:2],
            ordered,
            name="order",
            limit=6,
            input_output_aliases={3: 0},
        )
        places, last, choice = [2, 3], pieces[3][2:], choices[3]
    else:
        places, last, choice = list(range(blocks)), pieces[0], choices[0]

    tile_rows = 2 * inputs // blocks
    fine, gram = call(
        functools.partial(gram_kernel, blocks, relative, places),
        [shape((frames, 2 * inputs), jnp.bfloat16), shape((tile_rows, 2 * inputs), jnp.bfloat16)],
        choice,
        *last,
        ordered,
        name="gram",
        limit=20 if relative else 40,
        outs=HBM,
        scratch_shapes=[
            pltpu.VMEM(ordered_shape.shape, jnp.bfloat16),
            pltpu.VMEM((tile_rows, blocks * frames), jnp.bfloat16),
            pltpu.VMEM((tile_rows, 2 * inputs), jnp.bfloat16),
            pltpu.SemaphoreType.DMA((9,)),
        ],
    )
    return fine[None], gram[None]


def solution(mesh):
    placed = (P("chan", None, "grp", "tblk"), P("chan", None, "grp", None), P())
    return jax.shard_map(
        local,
        mesh=mesh,
        in_specs=placed,
        out_specs=(P(("grp", "chan"), "tblk", None), P(("grp", "chan"), "tblk", None)),
        check_vma=False,
    )
```

```python
import functools
import math

import jax
import jax.numpy as jnp
import numpy as np
from jax import lax
from jax.experimental import pallas as pl
from jax.experimental.pallas import tpu as pltpu
from jax.sharding import PartitionSpec as P

UPCHAN = 16
TAPS = 4
GROUP = 16
PAD = 128
MIB = 1 << 20
VMEM = pl.BlockSpec(memory_space=pltpu.VMEM)
HBM = pl.BlockSpec(memory_space=pltpu.HBM)
ANY = pl.BlockSpec(memory_space=pl.ANY)


def shifted(value, axis, steps):
    count = lax.axis_size(axis)
    leading, last = (max(0, -steps), min(count, count - steps))
    return lax.ppermute(value, axis, [(source, source + steps) for source in range(leading, last)])


def swapped(value, axis, distance):
    count = lax.axis_size(axis)
    return lax.ppermute(value, axis, [(source, source ^ distance) for source in range(count)])


def dot_samples(table, samples):
    return lax.dot_general(table, samples, (((1,), (1,)), ((), ())), preferred_element_type=jnp.float32)


def window_norm():
    length = TAPS * UPCHAN
    taps = np.arange(length)
    window = np.sinc((taps - (length - 1) / 2.0) / UPCHAN)
    window = window * (0.5 - 0.5 * np.cos(2.0 * math.pi * (taps + 0.5) / length))
    return float(1.0 / np.sqrt(np.sum(window * window)))


def windows(frames, width, offset):
    length = TAPS * UPCHAN
    shape = (frames, width)
    tap = lax.broadcasted_iota(jnp.int32, shape, 1) - offset - UPCHAN * lax.broadcasted_iota(jnp.int32, shape, 0)
    place = tap.astype(jnp.float32)
    u = (place - (length - 1) / 2.0) * (math.pi / UPCHAN)
    value = jnp.sin(u) / u * (0.5 - 0.5 * jnp.cos(2.0 * math.pi * (place + 0.5) / length)) * window_norm()
    return jnp.where((tap >= 0) & (tap < length), value, 0.0)


def group_table(bins, values, offset):
    frames, width = values.shape
    sample = lax.broadcasted_iota(jnp.int32, (8, PAD), 1)
    quarter = lax.broadcasted_iota(jnp.int32, (8, PAD), 0)
    rows = []
    for k in bins:
        turn = (k * sample + 4 * (quarter - 1)) % UPCHAN
        wave = jnp.cos(turn.astype(jnp.float32) * (2.0 * math.pi / UPCHAN))
        for out in range(2):
            tiles = []
            for lane in range(0, width, PAD):
                for part in range(2):
                    quarters = out - part + 1
                    tiles.append(values[:, lane : lane + PAD] * wave[quarters : quarters + 1, :])
            rows.append(jnp.concatenate(tiles, axis=1))
    table = jnp.concatenate(rows, axis=0)
    high = table.astype(jnp.bfloat16)
    low = (table - high.astype(jnp.float32)).astype(jnp.bfloat16)
    return jnp.concatenate([high, low], axis=0)


def both_halves(table, samples, contract=1):
    total = lax.dot_general(table, samples, (((1,), (contract,)), ((), ())), preferred_element_type=jnp.float32)
    return total[: total.shape[0] // 2] + total[total.shape[0] // 2 :]


def history_kernel(bins_per_coarse, lead_width, samples_ref, tail_ref, pairs_ref):
    values = windows(8, PAD, PAD - lead_width)
    at = 0
    for coarse, bins in enumerate(bins_per_coarse):
        table = group_table(range(bins), values, PAD - lead_width)
        samples = jnp.concatenate(parts_of(samples_ref, pairs_ref, coarse, 0), axis=1)
        total = both_halves(table, samples).reshape(bins, 2, 8, -1)[:, :, :4, :]
        tail_ref[at : at + bins * 8, :] = total.reshape(bins * 8, -1)
        at += bins * 8


def parts_of(samples_ref, pairs_ref, coarse, lane):
    slots = samples_ref.shape[0]
    pairs = samples_ref[:, coarse, :, lane : lane + PAD].reshape(2 * slots, PAD)
    place = lane * 2 * slots // PAD
    pairs_ref[place : place + 2 * slots, :] = pairs.astype(jnp.float32)
    return [pairs_ref[pl.ds(place + part, slots, stride=2), :].astype(jnp.bfloat16) for part in range(2)]


def channel_kernel(plan, lead_width, volts_ref, *refs):
    spectrum_refs, early_ref, pairs_ref = refs[:-2], refs[-2], refs[-1]
    slots, _, _, width = volts_ref.shape
    frames = width // UPCHAN
    groups = frames // GROUP
    span = PAD + GROUP * UPCHAN
    me = lax.axis_index("chan")
    values = windows(GROUP, span, PAD - lead_width)
    for coarse, members in plan:
        bins = [lax.bitwise_xor(me, distance) if relative else distance for relative, distance, _ in members]
        count = len(bins)
        table = group_table(bins, values, PAD - lead_width)
        samples = [
            jnp.concatenate(parts_of(volts_ref, pairs_ref, coarse, lane), axis=1) for lane in range(0, width, PAD)
        ]
        for group in range(groups):
            total = 0.0
            for lane in range(span // PAD):
                at = group * GROUP * UPCHAN // PAD - 1 + lane
                if at >= 0:
                    columns = slice(2 * lane * PAD, 2 * (lane + 1) * PAD)
                    total = total + both_halves(table[:, columns], samples[at])
            total = total.reshape(count, 2, GROUP, slots)
            if group == 0:
                row = (coarse * UPCHAN) * 8
                early_ref[row : row + count * 8, :] = total[:, :, :4, :].reshape(count * 8, slots)
            for at, (_, _, (out, index)) in enumerate(members):
                for part in range(2):
                    row = part * frames + group * GROUP
                    spectrum_refs[out][index, row : row + GROUP, :] = total[at, part].astype(jnp.bfloat16)


def early_kernel(plan, lead_ref, early_ref, history_ref, *refs):
    spectra_in, spectra_out = refs[: len(refs) // 2], refs[len(refs) // 2 :]
    lead_width, slots = lead_ref.shape[2:]
    first = lax.axis_index("tblk") == 0
    me = lax.axis_index("chan")
    values = windows(8, PAD, PAD - lead_width)
    for coarse, members in plan:
        bins = [lax.bitwise_xor(me, distance) if relative else distance for relative, distance, _ in members]
        table = group_table(bins, values, PAD - lead_width)
        lead = []
        for part in range(2):
            lead += [jnp.zeros((PAD - lead_width, slots), jnp.bfloat16), lead_ref[part, coarse, :, :]]
        head = both_halves(table, jnp.concatenate(lead, axis=0), 0).reshape(len(bins), 2, 8, slots)[:, :, :4, :]
        head = jnp.where(first, head.reshape(len(bins) * 8, slots), 0.0)
        for at, (relative, distance, (out, index)) in enumerate(members):
            frames = spectra_in[out].shape[1] // 2
            bin_at = bins[at] + coarse * UPCHAN
            row = (coarse * UPCHAN + at) * 8
            history = history_ref[pl.ds(pl.multiple_of(bin_at * 8, 8), 8), :]
            total = early_ref[row : row + 8, :] + history + head[at * 8 : (at + 1) * 8]
            for part in range(2):
                opening = total if part == 0 else pltpu.roll(total, 4, 0)
                opening = jnp.concatenate([opening, opening], axis=0)
                old = spectra_in[out][index, part * frames : part * frames + GROUP, :].astype(jnp.float32)
                row = lax.broadcasted_iota(jnp.int32, old.shape, 0)
                new = jnp.where(row < 4, opening, old).astype(jnp.bfloat16)
                spectra_out[out][index, part * frames : part * frames + GROUP, :] = new


def choice_kernel(relative, source, slots, slot_ref, choice_ref):
    owner = lax.bitwise_xor(lax.axis_index("chan"), source) if relative else source
    for row in range(0, choice_ref.shape[0], 64):
        rows = min(64, choice_ref.shape[0] - row)
        place = lax.broadcasted_iota(jnp.int32, (rows, slot_ref.shape[1]), 0) + (owner * slots + row)
        choice_ref[row : row + rows, :] = (place == slot_ref[...]).astype(jnp.bfloat16)


def order_kernel(rows, places, fresh, choice_ref, *refs):
    pieces, new_ref = refs[: len(places)], refs[-1]
    put_in_order(rows, places, fresh, choice_ref, pieces, refs[-2], new_ref)


def put_in_order(rows, places, fresh, choice_ref, pieces, old_ref, new_ref):
    frames = rows // 2
    inputs = choice_ref.shape[1]
    stacked = [piece[at * rows : (at + 1) * rows, :] for piece, (_, at) in zip(pieces, places)]
    stacked = jnp.concatenate(stacked, axis=0)
    for column in range(0, inputs, 256):
        total = jnp.dot(stacked, choice_ref[:, column : column + 256], preferred_element_type=jnp.float32)
        total = total.astype(jnp.bfloat16)
        for at, (place, _) in enumerate(places):
            for part in range(2):
                value = total[at * rows + part * frames : at * rows + (part + 1) * frames]
                to = (slice(place * frames, (place + 1) * frames), slice(part * inputs + column, part * inputs + column + 256))
                new_ref[to] = value if fresh else old_ref[to] + value


def after(value, *others):
    return call(
        lambda *refs: None,
        jax.ShapeDtypeStruct(value.shape, value.dtype),
        value,
        *others,
        name="after",
        limit=1,
        spaces=ANY,
        outs=ANY,
        input_output_aliases={0: 0},
    )


def join_kernel(*refs):
    rows = refs[0].shape[0]
    for at, ref in enumerate(refs[:-1]):
        refs[-1][at * rows : (at + 1) * rows, :] = ref[...]


def from_other_core(parts):
    rows, slots = parts[0].shape
    if len(parts) == 1:
        return [(swapped(parts[0], "tblk", 1), 0)]
    joined = call(
        join_kernel, jax.ShapeDtypeStruct((len(parts) * rows, slots), parts[0].dtype), *parts, name="join", limit=4
    )
    other = swapped(joined, "tblk", 1)
    return [(other, at) for at in range(len(parts))]


def gram_kernel(blocks, relative, *refs):
    parts = refs[:-6]
    fine_hbm, gram_hbm, ordered, tile, result, sems = refs[-6:]
    frames = ordered.shape[0] // blocks
    width = tile.shape[0]
    own = 0 if relative else pl.multiple_of(lax.axis_index("tblk") * frames, frames)
    copies = [pltpu.make_async_copy(parts[0].at[pl.ds(own, frames), :], fine_hbm, sems.at[0])]
    copies[0].start()
    row = 0
    for part in parts:
        ordered[row : row + part.shape[0], :] = part[...]
        row += part.shape[0]
    place = pl.multiple_of(lax.axis_index("tblk") * width, width)
    tile[...] = ordered[:, pl.ds(place, width)].T
    chunk = width // 8
    for at in range(8):
        rows = slice(at * chunk, (at + 1) * chunk)
        gram = jnp.dot(tile[rows, :], ordered[...], preferred_element_type=jnp.float32)
        result[rows, :] = (gram * (1.0 / ordered.shape[0])).astype(jnp.bfloat16)
        copy = pltpu.make_async_copy(
            result.at[pl.ds(at * chunk, chunk), :], gram_hbm.at[pl.ds(at * chunk, chunk), :], sems.at[at + 1]
        )
        copy.start()
        copies.append(copy)
    for copy in copies:
        copy.wait()


def call(kernel, shapes, *operands, name, limit, spaces=VMEM, outs=VMEM, flops=0, moved=0, **options):
    spaces = spaces if isinstance(spaces, list) else [spaces] * len(operands)
    several = isinstance(shapes, list)
    return pl.pallas_call(
        kernel,
        in_specs=spaces,
        out_specs=[outs] * len(shapes) if several else outs,
        out_shape=shapes,
        compiler_params=pltpu.CompilerParams(vmem_limit_bytes=limit * MIB),
        name=name,
        cost_estimate=pl.CostEstimate(flops=flops, bytes_accessed=moved, transcendentals=0),
        **options,
    )(*operands)


def local(coarse_volts, lead_in, slot_of_input):
    slots, _, coarse, width = coarse_volts.shape
    lead_width = lead_in.shape[3]
    chans, blocks = lax.axis_size("chan"), lax.axis_size("tblk")
    frames = width // UPCHAN
    inputs = slot_of_input.shape[0]
    relative = coarse == 1 and chans == 4 and blocks == 4
    volts = coarse_volts.transpose(0, 2, 1, 3)
    lead = lead_in.transpose(1, 2, 3, 0)
    order = slot_of_input.reshape(1, inputs)

    per_coarse = [max(0, min(UPCHAN, chans - c * UPCHAN)) for c in range(coarse)]
    shape = jax.ShapeDtypeStruct

    opening = call(
        functools.partial(history_kernel, per_coarse, lead_width),
        shape((chans * 8, slots), jnp.float32),
        volts,
        name="history",
        moved=2 * MIB,
        limit=4,
        grid=(1,),
        spaces=[pl.BlockSpec((slots, coarse, 2, PAD), lambda i: (0, 0, 0, width // PAD - 1))],
        outs=pl.BlockSpec((chans * 8, slots), lambda i: (0, 0)),
        scratch_shapes=[pltpu.VMEM((2 * slots, PAD), jnp.float32)],
    )
    history = shifted(opening, "tblk", 1)

    if relative:
        plan = [(0, [(True, distance, (distance, 0)) for distance in range(chans)])]
        shapes = [shape((1, 2 * frames, slots), jnp.bfloat16)] * chans
    else:
        plan = [
            (c, [(False, k, (0, c * UPCHAN + k)) for k in range(count)]) for c, count in enumerate(per_coarse) if count
        ]
        shapes = [shape((chans, 2 * frames, slots), jnp.bfloat16)]
    *spectra, early = call(
        functools.partial(channel_kernel, plan, lead_width),
        shapes + [shape((chans * 8, slots), jnp.float32)],
        volts,
        name="channelize",
        moved=6 * MIB,
        limit=14,
        scratch_shapes=[pltpu.VMEM((2 * slots * width // PAD, PAD), jnp.float32)],
    )
    spectra = call(
        functools.partial(early_kernel, plan),
        shapes,
        lead,
        early,
        history,
        *spectra,
        name="early",
        limit=2,
        input_output_aliases={3 + at: at for at in range(len(shapes))},
    )

    sources = range(chans) if relative else [0]
    wide = slots if relative else inputs
    choices = [
        call(
            functools.partial(choice_kernel, relative, source, wide),
            shape((wide, inputs), jnp.bfloat16),
            order,
            name="choice",
            moved=2 * wide * inputs,
            limit=2 if relative else 10,
        )
        for source in sources
    ]
    mine = blocks // 2 if relative else blocks
    ordered_shape = shape((mine * frames, 2 * inputs), jnp.bfloat16)

    def put(source, given, ordered):
        given = [(to, *piece) for to, piece in given]
        old = [] if ordered is None else [ordered]
        return call(
            functools.partial(order_kernel, 2 * frames, [(to, at) for to, _, at in given], ordered is None),
            ordered_shape,
            choices[source],
            *[array for _, array, _ in given],
            *old,
            name="order",
            flops=4 * len(given) * frames * wide * inputs,
            limit=6 if relative else 24,
            input_output_aliases={1 + len(given): 0} if old else {},
        )

    if relative:
        spectra = [s[0] for s in spectra]
        own, one = spectra[0], spectra[1]
        z2, z3 = swapped(spectra[2], "chan", 2), swapped(spectra[3], "chan", 3)
        z1 = swapped(one, "chan", 1)
        x1 = lax.ppermute(
            one,
            ("chan", "tblk"),
            [(c * blocks + b, (c ^ 1) * blocks + (b ^ 2)) for c in range(chans) for b in range(blocks)],
        )
        x0 = swapped(own, "tblk", 2)
        x3 = swapped(z3, "tblk", 2)
        x2 = swapped(z2, "tblk", 2)
        ordered = put(0, [(0, (own, 0)), (1, (x0, 0))], None)
        ordered = put(1, [(0, (z1, 0)), (1, (x1, 0))], ordered)
        ordered = put(3, [(0, (z3, 0)), (1, (x3, 0))], ordered)
        ordered = put(2, [(0, (z2, 0)), (1, (x2, 0))], ordered)
        halves = [ordered, swapped(ordered, "tblk", 1)]
    else:
        owned = lax.all_to_all(spectra[0], "chan", split_axis=0, concat_axis=2, tiled=True)[0]
        all_time = lax.all_gather(owned, "tblk", axis=0)
        halves = [put(0, [(b, (all_time[b], 0)) for b in range(blocks)], None)]

    tile_rows = 2 * inputs // blocks
    fine, gram = call(
        functools.partial(gram_kernel, blocks, relative),
        [shape((frames, 2 * inputs), jnp.bfloat16), shape((tile_rows, 2 * inputs), jnp.bfloat16)],
        *halves,
        name="gram",
        moved=12 * MIB,
        limit=20 if relative else 40,
        outs=HBM,
        scratch_shapes=[
            pltpu.VMEM((blocks * frames, 2 * inputs), jnp.bfloat16),
            pltpu.VMEM((tile_rows, blocks * frames), jnp.bfloat16),
            pltpu.VMEM((tile_rows, 2 * inputs), jnp.bfloat16),
            pltpu.SemaphoreType.DMA((9,)),
        ],
    )
    return fine[None], gram[None]


def solution(mesh):
    placed = (P("chan", None, "grp", "tblk"), P("chan", None, "grp", None), P())
    return jax.shard_map(
        local,
        mesh=mesh,
        in_specs=placed,
        out_specs=(P(("grp", "chan"), "tblk", None), P(("grp", "chan"), "tblk", None)),
        check_vma=False,
    )
```

```python
import functools
import math

import jax
import jax.numpy as jnp
import numpy as np
from jax import lax
from jax.experimental import pallas as pl
from jax.experimental.pallas import tpu as pltpu
from jax.sharding import PartitionSpec as P

UPCHAN = 16
TAPS = 4
GROUP = 16
PAD = 128
MIB = 1 << 20
VMEM = pl.BlockSpec(memory_space=pltpu.VMEM)
HBM = pl.BlockSpec(memory_space=pltpu.HBM)
ANY = pl.BlockSpec(memory_space=pl.ANY)


def shifted(value, axis, steps):
    count = lax.axis_size(axis)
    leading, last = (max(0, -steps), min(count, count - steps))
    return lax.ppermute(value, axis, [(source, source + steps) for source in range(leading, last)])


def swapped(value, axis, distance):
    count = lax.axis_size(axis)
    return lax.ppermute(value, axis, [(source, source ^ distance) for source in range(count)])


def dot_samples(table, samples):
    return lax.dot_general(table, samples, (((1,), (1,)), ((), ())), preferred_element_type=jnp.float32)


def window_norm():
    length = TAPS * UPCHAN
    taps = np.arange(length)
    window = np.sinc((taps - (length - 1) / 2.0) / UPCHAN)
    window = window * (0.5 - 0.5 * np.cos(2.0 * math.pi * (taps + 0.5) / length))
    return float(1.0 / np.sqrt(np.sum(window * window)))


def windows(frames, width, offset):
    length = TAPS * UPCHAN
    shape = (frames, width)
    tap = lax.broadcasted_iota(jnp.int32, shape, 1) - offset - UPCHAN * lax.broadcasted_iota(jnp.int32, shape, 0)
    place = tap.astype(jnp.float32)
    u = (place - (length - 1) / 2.0) * (math.pi / UPCHAN)
    value = jnp.sin(u) / u * (0.5 - 0.5 * jnp.cos(2.0 * math.pi * (place + 0.5) / length)) * window_norm()
    return jnp.where((tap >= 0) & (tap < length), value, 0.0)


def group_table(bins, values, offset):
    frames, width = values.shape
    sample = lax.broadcasted_iota(jnp.int32, (8, PAD), 1)
    quarter = lax.broadcasted_iota(jnp.int32, (8, PAD), 0)
    rows = []
    for k in bins:
        turn = (k * sample + 4 * (quarter - 1)) % UPCHAN
        wave = jnp.cos(turn.astype(jnp.float32) * (2.0 * math.pi / UPCHAN))
        for out in range(2):
            tiles = []
            for lane in range(0, width, PAD):
                for part in range(2):
                    quarters = out - part + 1
                    tiles.append(values[:, lane : lane + PAD] * wave[quarters : quarters + 1, :])
            rows.append(jnp.concatenate(tiles, axis=1))
    table = jnp.concatenate(rows, axis=0)
    high = table.astype(jnp.bfloat16)
    low = (table - high.astype(jnp.float32)).astype(jnp.bfloat16)
    return jnp.concatenate([high, low], axis=0)


def both_halves(table, samples, contract=1):
    total = lax.dot_general(table, samples, (((1,), (contract,)), ((), ())), preferred_element_type=jnp.float32)
    return total[: total.shape[0] // 2] + total[total.shape[0] // 2 :]


def history_kernel(bins_per_coarse, lead_width, volts_ref, tail_ref, pairs_ref):
    width = volts_ref.shape[3]
    values = windows(8, PAD, PAD - lead_width)
    at = 0
    for coarse, bins in enumerate(bins_per_coarse):
        table = group_table(range(bins), values, PAD - lead_width)
        samples = jnp.concatenate(parts_of(volts_ref, pairs_ref, coarse, width - PAD, 0), axis=1)
        total = both_halves(table, samples).reshape(bins, 2, 8, -1)[:, :, :4, :]
        tail_ref[at : at + bins * 8, :] = total.reshape(bins * 8, -1)
        at += bins * 8


def parts_of(samples_ref, pairs_ref, coarse, lane, place=None):
    slots = samples_ref.shape[0]
    pairs = samples_ref[:, coarse, :, lane : lane + PAD].reshape(2 * slots, PAD)
    place = lane * 2 * slots // PAD if place is None else place
    pairs_ref[place : place + 2 * slots, :] = pairs.astype(jnp.float32)
    return [pairs_ref[pl.ds(place + part, slots, stride=2), :].astype(jnp.bfloat16) for part in range(2)]


def channel_kernel(plan, lead_width, volts_ref, *refs):
    spectrum_refs, early_ref, pairs_ref = refs[:-2], refs[-2], refs[-1]
    slots, _, _, width = volts_ref.shape
    frames = width // UPCHAN
    groups = frames // GROUP
    span = PAD + GROUP * UPCHAN
    me = lax.axis_index("chan")
    values = windows(GROUP, span, PAD - lead_width)
    for coarse, members in plan:
        bins = [lax.bitwise_xor(me, distance) if relative else distance for relative, distance, _ in members]
        count = len(bins)
        table = group_table(bins, values, PAD - lead_width)
        samples = [
            jnp.concatenate(parts_of(volts_ref, pairs_ref, coarse, lane), axis=1) for lane in range(0, width, PAD)
        ]
        for group in range(groups):
            total = 0.0
            for lane in range(span // PAD):
                at = group * GROUP * UPCHAN // PAD - 1 + lane
                if at >= 0:
                    columns = slice(2 * lane * PAD, 2 * (lane + 1) * PAD)
                    total = total + both_halves(table[:, columns], samples[at])
            total = total.reshape(count, 2, GROUP, slots)
            if group == 0:
                row = (coarse * UPCHAN) * 8
                early_ref[row : row + count * 8, :] = total[:, :, :4, :].reshape(count * 8, slots)
            for at, (_, _, (out, index)) in enumerate(members):
                for part in range(2):
                    row = part * frames + group * GROUP
                    spectrum_refs[out][index, row : row + GROUP, :] = total[at, part].astype(jnp.bfloat16)


def early_kernel(plan, lead_ref, early_ref, history_ref, *refs):
    head_ref, refs = refs[-1], refs[:-1]
    spectra_in, spectra_out = refs[: len(refs) // 2], refs[len(refs) // 2 :]
    lead_width, slots = lead_ref.shape[2:]
    first = lax.axis_index("tblk") == 0
    me = lax.axis_index("chan")
    head_ref[...] = jnp.zeros_like(head_ref)

    @pl.when(first)
    def _():
        values = windows(8, PAD, PAD - lead_width)
        for coarse, members in plan:
            bins = [lax.bitwise_xor(me, distance) if relative else distance for relative, distance, _ in members]
            table = group_table(bins, values, PAD - lead_width)
            lead = []
            for part in range(2):
                lead += [jnp.zeros((PAD - lead_width, slots), jnp.bfloat16), lead_ref[part, coarse, :, :]]
            head = both_halves(table, jnp.concatenate(lead, axis=0), 0).reshape(len(bins), 2, 8, slots)[:, :, :4, :]
            row = coarse * UPCHAN * 8
            head_ref[row : row + len(bins) * 8, :] = head.reshape(len(bins) * 8, slots)

    for coarse, members in plan:
        bins = [lax.bitwise_xor(me, distance) if relative else distance for relative, distance, _ in members]
        for at, (relative, distance, (out, index)) in enumerate(members):
            frames = spectra_in[out].shape[1] // 2
            bin_at = bins[at] + coarse * UPCHAN
            row = (coarse * UPCHAN + at) * 8
            history = history_ref[pl.ds(pl.multiple_of(bin_at * 8, 8), 8), :]
            total = early_ref[row : row + 8, :] + history + head_ref[row : row + 8, :]
            for part in range(2):
                opening = total if part == 0 else pltpu.roll(total, 4, 0)
                opening = jnp.concatenate([opening, opening], axis=0)
                old = spectra_in[out][index, part * frames : part * frames + GROUP, :].astype(jnp.float32)
                row = lax.broadcasted_iota(jnp.int32, old.shape, 0)
                new = jnp.where(row < 4, opening, old).astype(jnp.bfloat16)
                spectra_out[out][index, part * frames : part * frames + GROUP, :] = new


def choice_kernel(relative, source, slots, slot_ref, choice_ref):
    owner = lax.bitwise_xor(lax.axis_index("chan"), source) if relative else source
    for row in range(0, choice_ref.shape[0], 64):
        rows = min(64, choice_ref.shape[0] - row)
        place = lax.broadcasted_iota(jnp.int32, (rows, slot_ref.shape[1]), 0) + (owner * slots + row)
        choice_ref[row : row + rows, :] = (place == slot_ref[...]).astype(jnp.bfloat16)


def order_kernel(rows, places, fresh, choice_ref, *refs):
    pieces, new_ref = refs[: len(places)], refs[-1]
    put_in_order(rows, places, fresh, choice_ref, pieces, refs[-2], new_ref)


def put_in_order(rows, places, fresh, choice_ref, pieces, old_ref, new_ref):
    frames = rows // 2
    inputs = choice_ref.shape[1]
    stacked = [piece[at * rows : (at + 1) * rows, :] for piece, (_, at) in zip(pieces, places)]
    stacked = jnp.concatenate(stacked, axis=0)
    for column in range(0, inputs, 256):
        total = jnp.dot(stacked, choice_ref[:, column : column + 256], preferred_element_type=jnp.float32)
        total = total.astype(jnp.bfloat16)
        for at, (place, _) in enumerate(places):
            for part in range(2):
                value = total[at * rows + part * frames : at * rows + (part + 1) * frames]
                to = (slice(place * frames, (place + 1) * frames), slice(part * inputs + column, part * inputs + column + 256))
                new_ref[to] = value if fresh else old_ref[to] + value


def after(value, *others):
    return call(
        lambda *refs: None,
        jax.ShapeDtypeStruct(value.shape, value.dtype),
        value,
        *others,
        name="after",
        limit=1,
        spaces=ANY,
        outs=ANY,
        input_output_aliases={0: 0},
    )


def join_kernel(*refs):
    rows = refs[0].shape[0]
    for at, ref in enumerate(refs[:-1]):
        refs[-1][at * rows : (at + 1) * rows, :] = ref[...]


def from_other_core(parts):
    rows, slots = parts[0].shape
    if len(parts) == 1:
        return [(swapped(parts[0], "tblk", 1), 0)]
    joined = call(
        join_kernel, jax.ShapeDtypeStruct((len(parts) * rows, slots), parts[0].dtype), *parts, name="join", limit=4
    )
    other = swapped(joined, "tblk", 1)
    return [(other, at) for at in range(len(parts))]


def gram_kernel(blocks, relative, *refs):
    parts = refs[:-6]
    fine_hbm, gram_hbm, ordered, tile, result, sems = refs[-6:]
    frames = ordered.shape[0] // blocks
    width = tile.shape[0]
    own = 0 if relative else pl.multiple_of(lax.axis_index("tblk") * frames, frames)
    copies = [pltpu.make_async_copy(parts[0].at[pl.ds(own, frames), :], fine_hbm, sems.at[0])]
    copies[0].start()
    row = 0
    for part in parts:
        ordered[row : row + part.shape[0], :] = part[...]
        row += part.shape[0]
    place = pl.multiple_of(lax.axis_index("tblk") * width, width)
    tile[...] = ordered[:, pl.ds(place, width)].T
    chunk = width // 8
    for at in range(8):
        rows = slice(at * chunk, (at + 1) * chunk)
        gram = jnp.dot(tile[rows, :], ordered[...], preferred_element_type=jnp.float32)
        result[rows, :] = (gram * (1.0 / ordered.shape[0])).astype(jnp.bfloat16)
        copy = pltpu.make_async_copy(
            result.at[pl.ds(at * chunk, chunk), :], gram_hbm.at[pl.ds(at * chunk, chunk), :], sems.at[at + 1]
        )
        copy.start()
        copies.append(copy)
    for copy in copies:
        copy.wait()


def call(kernel, shapes, *operands, name, limit, spaces=VMEM, outs=VMEM, flops=0, moved=0, **options):
    spaces = spaces if isinstance(spaces, list) else [spaces] * len(operands)
    several = isinstance(shapes, list)
    return pl.pallas_call(
        kernel,
        in_specs=spaces,
        out_specs=[outs] * len(shapes) if several else outs,
        out_shape=shapes,
        compiler_params=pltpu.CompilerParams(vmem_limit_bytes=limit * MIB),
        name=name,
        cost_estimate=pl.CostEstimate(flops=flops, bytes_accessed=moved, transcendentals=0),
        **options,
    )(*operands)


def local(coarse_volts, lead_in, slot_of_input):
    slots, _, coarse, width = coarse_volts.shape
    lead_width = lead_in.shape[3]
    chans, blocks = lax.axis_size("chan"), lax.axis_size("tblk")
    frames = width // UPCHAN
    inputs = slot_of_input.shape[0]
    relative = coarse == 1 and chans == 4 and blocks == 4
    volts = coarse_volts.transpose(0, 2, 1, 3)
    lead = lead_in.transpose(1, 2, 3, 0)
    order = slot_of_input.reshape(1, inputs)

    per_coarse = [max(0, min(UPCHAN, chans - c * UPCHAN)) for c in range(coarse)]
    shape = jax.ShapeDtypeStruct

    opening = call(
        functools.partial(history_kernel, per_coarse, lead_width),
        shape((chans * 8, slots), jnp.float32),
        volts,
        name="history",
        moved=2 * MIB,
        limit=4,
        scratch_shapes=[pltpu.VMEM((2 * slots, PAD), jnp.float32)],
    )
    history = shifted(opening, "tblk", 1)

    if relative:
        plan = [(0, [(True, distance, (distance, 0)) for distance in range(chans)])]
        shapes = [shape((1, 2 * frames, slots), jnp.bfloat16)] * chans
    else:
        plan = [
            (c, [(False, k, (0, c * UPCHAN + k)) for k in range(count)]) for c, count in enumerate(per_coarse) if count
        ]
        shapes = [shape((chans, 2 * frames, slots), jnp.bfloat16)]
    *spectra, early = call(
        functools.partial(channel_kernel, plan, lead_width),
        shapes + [shape((chans * 8, slots), jnp.float32)],
        volts,
        name="channelize",
        moved=6 * MIB,
        limit=14,
        scratch_shapes=[pltpu.VMEM((2 * slots * width // PAD, PAD), jnp.float32)],
    )
    spectra = call(
        functools.partial(early_kernel, plan),
        shapes,
        lead,
        early,
        history,
        *spectra,
        name="early",
        limit=2,
        scratch_shapes=[pltpu.VMEM((chans * 8, slots), jnp.float32)],
        input_output_aliases={3 + at: at for at in range(len(shapes))},
    )

    sources = range(chans) if relative else [0]
    wide = slots if relative else inputs
    choices = [
        call(
            functools.partial(choice_kernel, relative, source, wide),
            shape((wide, inputs), jnp.bfloat16),
            order,
            name="choice",
            moved=0,
            limit=2 if relative else 10,
        )
        for source in sources
    ]
    mine = blocks // 2 if relative else blocks
    ordered_shape = shape((mine * frames, 2 * inputs), jnp.bfloat16)

    def put(source, given, ordered):
        given = [(to, *piece) for to, piece in given]
        old = [] if ordered is None else [ordered]
        return call(
            functools.partial(order_kernel, 2 * frames, [(to, at) for to, _, at in given], ordered is None),
            ordered_shape,
            choices[source],
            *[array for _, array, _ in given],
            *old,
            name="order",
            flops=4 * len(given) * frames * wide * inputs,
            limit=6 if relative else 24,
            input_output_aliases={1 + len(given): 0} if old else {},
        )

    if relative:
        spectra = [s[0] for s in spectra]
        own, one = spectra[0], spectra[1]
        z2, z3 = swapped(spectra[2], "chan", 2), swapped(spectra[3], "chan", 3)
        z1 = swapped(one, "chan", 1)
        x1 = lax.ppermute(
            one,
            ("chan", "tblk"),
            [(c * blocks + b, (c ^ 1) * blocks + (b ^ 2)) for c in range(chans) for b in range(blocks)],
        )
        x0 = swapped(own, "tblk", 2)
        x3 = swapped(z3, "tblk", 2)
        x2 = swapped(z2, "tblk", 2)
        ordered = put(1, [(0, (z1, 0)), (1, (x1, 0))], None)
        ordered = put(0, [(0, (own, 0)), (1, (x0, 0))], ordered)
        ordered = put(2, [(0, (z2, 0)), (1, (x2, 0))], ordered)
        ordered = put(3, [(0, (z3, 0)), (1, (x3, 0))], ordered)
        halves = [ordered, swapped(ordered, "tblk", 1)]
    else:
        owned = lax.all_to_all(spectra[0], "chan", split_axis=0, concat_axis=2, tiled=True)[0]
        all_time = lax.all_gather(owned, "tblk", axis=0)
        halves = [put(0, [(b, (all_time[b], 0)) for b in range(blocks)], None)]

    tile_rows = 2 * inputs // blocks
    fine, gram = call(
        functools.partial(gram_kernel, blocks, relative),
        [shape((frames, 2 * inputs), jnp.bfloat16), shape((tile_rows, 2 * inputs), jnp.bfloat16)],
        *halves,
        name="gram",
        moved=12 * MIB,
        limit=20 if relative else 40,
        outs=HBM,
        scratch_shapes=[
            pltpu.VMEM((blocks * frames, 2 * inputs), jnp.bfloat16),
            pltpu.VMEM((tile_rows, blocks * frames), jnp.bfloat16),
            pltpu.VMEM((tile_rows, 2 * inputs), jnp.bfloat16),
            pltpu.SemaphoreType.DMA((9,)),
        ],
    )
    return fine[None], gram[None]


def solution(mesh):
    placed = (P("chan", None, "grp", "tblk"), P("chan", None, "grp", None), P())
    return jax.shard_map(
        local,
        mesh=mesh,
        in_specs=placed,
        out_specs=(P(("grp", "chan"), "tblk", None), P(("grp", "chan"), "tblk", None)),
        check_vma=False,
    )
```

```python
import functools
import math

import jax
import jax.numpy as jnp
import numpy as np
from jax import lax
from jax.experimental import pallas as pl
from jax.experimental.pallas import tpu as pltpu
from jax.sharding import PartitionSpec as P

UPCHAN = 16
TAPS = 4
GROUP = 16
PAD = 128
MIB = 1 << 20
VMEM = pl.BlockSpec(memory_space=pltpu.VMEM)
HBM = pl.BlockSpec(memory_space=pltpu.HBM)
ANY = pl.BlockSpec(memory_space=pl.ANY)


def shifted(value, axis, steps):
    count = lax.axis_size(axis)
    leading, last = (max(0, -steps), min(count, count - steps))
    return lax.ppermute(value, axis, [(source, source + steps) for source in range(leading, last)])


def swapped(value, axis, distance):
    count = lax.axis_size(axis)
    return lax.ppermute(value, axis, [(source, source ^ distance) for source in range(count)])


def dot_samples(table, samples):
    return lax.dot_general(table, samples, (((1,), (1,)), ((), ())), preferred_element_type=jnp.float32)


def window_norm():
    length = TAPS * UPCHAN
    taps = np.arange(length)
    window = np.sinc((taps - (length - 1) / 2.0) / UPCHAN)
    window = window * (0.5 - 0.5 * np.cos(2.0 * math.pi * (taps + 0.5) / length))
    return float(1.0 / np.sqrt(np.sum(window * window)))


def windows(frames, width, offset):
    length = TAPS * UPCHAN
    shape = (frames, width)
    tap = lax.broadcasted_iota(jnp.int32, shape, 1) - offset - UPCHAN * lax.broadcasted_iota(jnp.int32, shape, 0)
    place = tap.astype(jnp.float32)
    u = (place - (length - 1) / 2.0) * (math.pi / UPCHAN)
    value = jnp.sin(u) / u * (0.5 - 0.5 * jnp.cos(2.0 * math.pi * (place + 0.5) / length)) * window_norm()
    return jnp.where((tap >= 0) & (tap < length), value, 0.0)


def group_table(bins, values, offset):
    frames, width = values.shape
    sample = lax.broadcasted_iota(jnp.int32, (8, PAD), 1)
    quarter = lax.broadcasted_iota(jnp.int32, (8, PAD), 0)
    rows = []
    for k in bins:
        turn = (k * sample + 4 * (quarter - 1)) % UPCHAN
        wave = jnp.cos(turn.astype(jnp.float32) * (2.0 * math.pi / UPCHAN))
        for out in range(2):
            tiles = []
            for lane in range(0, width, PAD):
                for part in range(2):
                    quarters = out - part + 1
                    tiles.append(values[:, lane : lane + PAD] * wave[quarters : quarters + 1, :])
            rows.append(jnp.concatenate(tiles, axis=1))
    table = jnp.concatenate(rows, axis=0)
    high = table.astype(jnp.bfloat16)
    low = (table - high.astype(jnp.float32)).astype(jnp.bfloat16)
    return jnp.concatenate([high, low], axis=0)


def both_halves(table, samples, contract=1):
    total = lax.dot_general(table, samples, (((1,), (contract,)), ((), ())), preferred_element_type=jnp.float32)
    return total[: total.shape[0] // 2] + total[total.shape[0] // 2 :]


def history_kernel(bins_per_coarse, lead_width, volts_ref, tail_ref, pairs_ref):
    width = volts_ref.shape[3]
    values = windows(8, PAD, PAD - lead_width)
    at = 0
    for coarse, bins in enumerate(bins_per_coarse):
        table = group_table(range(bins), values, PAD - lead_width)
        samples = jnp.concatenate(parts_of(volts_ref, pairs_ref, coarse, width - PAD, 0), axis=1)
        total = both_halves(table, samples).reshape(bins, 2, 8, -1)[:, :, :4, :]
        tail_ref[at : at + bins * 8, :] = total.reshape(bins * 8, -1)
        at += bins * 8


def parts_of(samples_ref, pairs_ref, coarse, lane, place=None):
    slots = samples_ref.shape[0]
    pairs = samples_ref[:, coarse, :, lane : lane + PAD].reshape(2 * slots, PAD)
    place = lane * 2 * slots // PAD if place is None else place
    pairs_ref[place : place + 2 * slots, :] = pairs.astype(jnp.float32)
    return [pairs_ref[pl.ds(place + part, slots, stride=2), :].astype(jnp.bfloat16) for part in range(2)]


def channel_kernel(plan, lead_width, volts_ref, *refs):
    spectrum_refs, early_ref, pairs_ref = refs[:-2], refs[-2], refs[-1]
    slots, _, _, width = volts_ref.shape
    frames = width // UPCHAN
    groups = frames // GROUP
    span = PAD + GROUP * UPCHAN
    me = lax.axis_index("chan")
    values = windows(GROUP, span, PAD - lead_width)
    for coarse, members in plan:
        bins = [lax.bitwise_xor(me, distance) if relative else distance for relative, distance, _ in members]
        count = len(bins)
        table = group_table(bins, values, PAD - lead_width)
        samples = [
            jnp.concatenate(parts_of(volts_ref, pairs_ref, coarse, lane), axis=1) for lane in range(0, width, PAD)
        ]
        for group in range(groups):
            total = 0.0
            for lane in range(span // PAD):
                at = group * GROUP * UPCHAN // PAD - 1 + lane
                if at >= 0:
                    columns = slice(2 * lane * PAD, 2 * (lane + 1) * PAD)
                    total = total + both_halves(table[:, columns], samples[at])
            total = total.reshape(count, 2, GROUP, slots)
            if group == 0:
                row = (coarse * UPCHAN) * 8
                early_ref[row : row + count * 8, :] = total[:, :, :4, :].reshape(count * 8, slots)
            for at, (_, _, (out, index)) in enumerate(members):
                for part in range(2):
                    row = part * frames + group * GROUP
                    spectrum_refs[out][index, row : row + GROUP, :] = total[at, part].astype(jnp.bfloat16)


def early_kernel(plan, lead_ref, early_ref, history_ref, *refs):
    head_ref, refs = refs[-1], refs[:-1]
    spectra_in, spectra_out = refs[: len(refs) // 2], refs[len(refs) // 2 :]
    lead_width, slots = lead_ref.shape[2:]
    first = lax.axis_index("tblk") == 0
    me = lax.axis_index("chan")
    head_ref[...] = jnp.zeros_like(head_ref)

    @pl.when(first)
    def _():
        values = windows(8, PAD, PAD - lead_width)
        for coarse, members in plan:
            bins = [lax.bitwise_xor(me, distance) if relative else distance for relative, distance, _ in members]
            table = group_table(bins, values, PAD - lead_width)
            lead = []
            for part in range(2):
                lead += [jnp.zeros((PAD - lead_width, slots), jnp.bfloat16), lead_ref[part, coarse, :, :]]
            head = both_halves(table, jnp.concatenate(lead, axis=0), 0).reshape(len(bins), 2, 8, slots)[:, :, :4, :]
            row = coarse * UPCHAN * 8
            head_ref[row : row + len(bins) * 8, :] = head.reshape(len(bins) * 8, slots)

    for coarse, members in plan:
        bins = [lax.bitwise_xor(me, distance) if relative else distance for relative, distance, _ in members]
        for at, (relative, distance, (out, index)) in enumerate(members):
            frames = spectra_in[out].shape[1] // 2
            bin_at = bins[at] + coarse * UPCHAN
            row = (coarse * UPCHAN + at) * 8
            history = history_ref[pl.ds(pl.multiple_of(bin_at * 8, 8), 8), :]
            total = early_ref[row : row + 8, :] + history + head_ref[row : row + 8, :]
            for part in range(2):
                opening = total if part == 0 else pltpu.roll(total, 4, 0)
                opening = jnp.concatenate([opening, opening], axis=0)
                old = spectra_in[out][index, part * frames : part * frames + GROUP, :].astype(jnp.float32)
                row = lax.broadcasted_iota(jnp.int32, old.shape, 0)
                new = jnp.where(row < 4, opening, old).astype(jnp.bfloat16)
                spectra_out[out][index, part * frames : part * frames + GROUP, :] = new


def choice_kernel(relative, source, slots, slot_ref, choice_ref):
    owner = lax.bitwise_xor(lax.axis_index("chan"), source) if relative else source
    for row in range(0, choice_ref.shape[0], 64):
        rows = min(64, choice_ref.shape[0] - row)
        place = lax.broadcasted_iota(jnp.int32, (rows, slot_ref.shape[1]), 0) + (owner * slots + row)
        choice_ref[row : row + rows, :] = (place == slot_ref[...]).astype(jnp.bfloat16)


def order_kernel(rows, places, fresh, choice_ref, *refs):
    pieces, new_ref = refs[: len(places)], refs[-1]
    put_in_order(rows, places, fresh, choice_ref, pieces, refs[-2], new_ref)


def put_in_order(rows, places, fresh, choice_ref, pieces, old_ref, new_ref):
    frames = rows // 2
    inputs = choice_ref.shape[1]
    stacked = [piece[at * rows : (at + 1) * rows, :] for piece, (_, at) in zip(pieces, places)]
    stacked = jnp.concatenate(stacked, axis=0)
    for column in range(0, inputs, 256):
        total = jnp.dot(stacked, choice_ref[:, column : column + 256], preferred_element_type=jnp.float32)
        total = total.astype(jnp.bfloat16)
        for at, (place, _) in enumerate(places):
            for part in range(2):
                value = total[at * rows + part * frames : at * rows + (part + 1) * frames]
                to = (slice(place * frames, (place + 1) * frames), slice(part * inputs + column, part * inputs + column + 256))
                new_ref[to] = value if fresh else old_ref[to] + value


def after(value, *others):
    return call(
        lambda *refs: None,
        jax.ShapeDtypeStruct(value.shape, value.dtype),
        value,
        *others,
        name="after",
        limit=1,
        spaces=ANY,
        outs=ANY,
        input_output_aliases={0: 0},
    )


def join_kernel(*refs):
    rows = refs[0].shape[0]
    for at, ref in enumerate(refs[:-1]):
        refs[-1][at * rows : (at + 1) * rows, :] = ref[...]


def from_other_core(parts):
    rows, slots = parts[0].shape
    if len(parts) == 1:
        return [(swapped(parts[0], "tblk", 1), 0)]
    joined = call(
        join_kernel, jax.ShapeDtypeStruct((len(parts) * rows, slots), parts[0].dtype), *parts, name="join", limit=4
    )
    other = swapped(joined, "tblk", 1)
    return [(other, at) for at in range(len(parts))]


def gram_kernel(blocks, relative, *refs):
    parts = refs[:-6]
    fine_hbm, gram_hbm, ordered, tile, result, sems = refs[-6:]
    frames = ordered.shape[0] // blocks
    width = tile.shape[0]
    own = 0 if relative else pl.multiple_of(lax.axis_index("tblk") * frames, frames)
    copies = [pltpu.make_async_copy(parts[0].at[pl.ds(own, frames), :], fine_hbm, sems.at[0])]
    copies[0].start()
    row = 0
    for part in parts:
        ordered[row : row + part.shape[0], :] = part[...]
        row += part.shape[0]
    chunk = max(PAD, width // 8)
    for at in range(width // chunk):
        rows = slice(at * chunk, (at + 1) * chunk)
        place = pl.multiple_of(lax.axis_index("tblk") * width + at * chunk, chunk)
        tile[rows, :] = ordered[:, pl.ds(place, chunk)].T
        gram = jnp.dot(tile[rows, :], ordered[...], preferred_element_type=jnp.float32)
        result[rows, :] = (gram * (1.0 / ordered.shape[0])).astype(jnp.bfloat16)
        copy = pltpu.make_async_copy(
            result.at[pl.ds(at * chunk, chunk), :], gram_hbm.at[pl.ds(at * chunk, chunk), :], sems.at[at + 1]
        )
        copy.start()
        copies.append(copy)
    for copy in copies:
        copy.wait()


def call(kernel, shapes, *operands, name, limit, spaces=VMEM, outs=VMEM, flops=0, moved=0, **options):
    spaces = spaces if isinstance(spaces, list) else [spaces] * len(operands)
    several = isinstance(shapes, list)
    return pl.pallas_call(
        kernel,
        in_specs=spaces,
        out_specs=[outs] * len(shapes) if several else outs,
        out_shape=shapes,
        compiler_params=pltpu.CompilerParams(vmem_limit_bytes=limit * MIB),
        name=name,
        cost_estimate=pl.CostEstimate(flops=flops, bytes_accessed=moved, transcendentals=0),
        **options,
    )(*operands)


def local(coarse_volts, lead_in, slot_of_input):
    slots, _, coarse, width = coarse_volts.shape
    lead_width = lead_in.shape[3]
    chans, blocks = lax.axis_size("chan"), lax.axis_size("tblk")
    frames = width // UPCHAN
    inputs = slot_of_input.shape[0]
    relative = coarse == 1 and chans == 4 and blocks == 4
    volts = coarse_volts.transpose(0, 2, 1, 3)
    lead = lead_in.transpose(1, 2, 3, 0)
    order = slot_of_input.reshape(1, inputs)

    per_coarse = [max(0, min(UPCHAN, chans - c * UPCHAN)) for c in range(coarse)]
    shape = jax.ShapeDtypeStruct

    opening = call(
        functools.partial(history_kernel, per_coarse, lead_width),
        shape((chans * 8, slots), jnp.float32),
        volts,
        name="history",
        moved=2 * MIB,
        limit=4,
        scratch_shapes=[pltpu.VMEM((2 * slots, PAD), jnp.float32)],
    )
    history = shifted(opening, "tblk", 1)

    if relative:
        plan = [(0, [(True, distance, (distance, 0)) for distance in range(chans)])]
        shapes = [shape((1, 2 * frames, slots), jnp.bfloat16)] * chans
    else:
        plan = [
            (c, [(False, k, (0, c * UPCHAN + k)) for k in range(count)]) for c, count in enumerate(per_coarse) if count
        ]
        shapes = [shape((chans, 2 * frames, slots), jnp.bfloat16)]
    *spectra, early = call(
        functools.partial(channel_kernel, plan, lead_width),
        shapes + [shape((chans * 8, slots), jnp.float32)],
        volts,
        name="channelize",
        moved=6 * MIB,
        limit=14,
        scratch_shapes=[pltpu.VMEM((2 * slots * width // PAD, PAD), jnp.float32)],
    )
    spectra = call(
        functools.partial(early_kernel, plan),
        shapes,
        lead,
        early,
        history,
        *spectra,
        name="early",
        limit=2,
        scratch_shapes=[pltpu.VMEM((chans * 8, slots), jnp.float32)],
        input_output_aliases={3 + at: at for at in range(len(shapes))},
    )

    sources = range(chans) if relative else [0]
    wide = slots if relative else inputs
    choices = [
        call(
            functools.partial(choice_kernel, relative, source, wide),
            shape((wide, inputs), jnp.bfloat16),
            order,
            name="choice",
            moved=0,
            limit=2 if relative else 10,
        )
        for source in sources
    ]
    mine = blocks // 2 if relative else blocks
    ordered_shape = shape((mine * frames, 2 * inputs), jnp.bfloat16)

    def put(source, given, ordered):
        given = [(to, *piece) for to, piece in given]
        old = [] if ordered is None else [ordered]
        return call(
            functools.partial(order_kernel, 2 * frames, [(to, at) for to, _, at in given], ordered is None),
            ordered_shape,
            choices[source],
            *[array for _, array, _ in given],
            *old,
            name="order",
            flops=4 * len(given) * frames * wide * inputs,
            limit=6 if relative else 24,
            input_output_aliases={1 + len(given): 0} if old else {},
        )

    if relative:
        spectra = [s[0] for s in spectra]
        own, one = spectra[0], spectra[1]
        z2, z3 = swapped(spectra[2], "chan", 2), swapped(spectra[3], "chan", 3)
        z1 = swapped(one, "chan", 1)
        x1 = lax.ppermute(
            one,
            ("chan", "tblk"),
            [(c * blocks + b, (c ^ 1) * blocks + (b ^ 2)) for c in range(chans) for b in range(blocks)],
        )
        x0 = swapped(own, "tblk", 2)
        x3 = swapped(z3, "tblk", 2)
        x2 = swapped(z2, "tblk", 2)
        ordered = put(1, [(0, (z1, 0)), (1, (x1, 0))], None)
        ordered = put(0, [(0, (own, 0)), (1, (x0, 0))], ordered)
        ordered = put(2, [(0, (z2, 0)), (1, (x2, 0))], ordered)
        ordered = put(3, [(0, (z3, 0)), (1, (x3, 0))], ordered)
        halves = [ordered, swapped(ordered, "tblk", 1)]
    else:
        owned = lax.all_to_all(spectra[0], "chan", split_axis=0, concat_axis=2, tiled=True)[0]
        all_time = lax.all_gather(owned, "tblk", axis=0)
        halves = [put(0, [(b, (all_time[b], 0)) for b in range(blocks)], None)]

    tile_rows = 2 * inputs // blocks
    fine, gram = call(
        functools.partial(gram_kernel, blocks, relative),
        [shape((frames, 2 * inputs), jnp.bfloat16), shape((tile_rows, 2 * inputs), jnp.bfloat16)],
        *halves,
        name="gram",
        moved=12 * MIB,
        limit=20 if relative else 40,
        outs=HBM,
        scratch_shapes=[
            pltpu.VMEM((blocks * frames, 2 * inputs), jnp.bfloat16),
            pltpu.VMEM((tile_rows, blocks * frames), jnp.bfloat16),
            pltpu.VMEM((tile_rows, 2 * inputs), jnp.bfloat16),
            pltpu.SemaphoreType.DMA((9,)),
        ],
    )
    return fine[None], gram[None]


def solution(mesh):
    placed = (P("chan", None, "grp", "tblk"), P("chan", None, "grp", None), P())
    return jax.shard_map(
        local,
        mesh=mesh,
        in_specs=placed,
        out_specs=(P(("grp", "chan"), "tblk", None), P(("grp", "chan"), "tblk", None)),
        check_vma=False,
    )
```

```python
import functools
import math

import jax
import jax.numpy as jnp
import numpy as np
from jax import lax
from jax.experimental import pallas as pl
from jax.experimental.pallas import tpu as pltpu
from jax.sharding import PartitionSpec as P

UPCHAN = 16
TAPS = 4
GROUP = 16
PAD = 128
MIB = 1 << 20
VMEM = pl.BlockSpec(memory_space=pltpu.VMEM)
HBM = pl.BlockSpec(memory_space=pltpu.HBM)
ANY = pl.BlockSpec(memory_space=pl.ANY)


def shifted(value, axis, steps):
    count = lax.axis_size(axis)
    leading, last = (max(0, -steps), min(count, count - steps))
    return lax.ppermute(value, axis, [(source, source + steps) for source in range(leading, last)])


def swapped(value, axis, distance):
    count = lax.axis_size(axis)
    return lax.ppermute(value, axis, [(source, source ^ distance) for source in range(count)])


def dot_samples(table, samples):
    return lax.dot_general(table, samples, (((1,), (1,)), ((), ())), preferred_element_type=jnp.float32)


def window_norm():
    length = TAPS * UPCHAN
    taps = np.arange(length)
    window = np.sinc((taps - (length - 1) / 2.0) / UPCHAN)
    window = window * (0.5 - 0.5 * np.cos(2.0 * math.pi * (taps + 0.5) / length))
    return float(1.0 / np.sqrt(np.sum(window * window)))


def windows(frames, width, offset):
    length = TAPS * UPCHAN
    shape = (frames, width)
    tap = lax.broadcasted_iota(jnp.int32, shape, 1) - offset - UPCHAN * lax.broadcasted_iota(jnp.int32, shape, 0)
    place = tap.astype(jnp.float32)
    u = (place - (length - 1) / 2.0) * (math.pi / UPCHAN)
    value = jnp.sin(u) / u * (0.5 - 0.5 * jnp.cos(2.0 * math.pi * (place + 0.5) / length)) * window_norm()
    return jnp.where((tap >= 0) & (tap < length), value, 0.0)


def group_table(bins, values, offset):
    frames, width = values.shape
    sample = lax.broadcasted_iota(jnp.int32, (8, PAD), 1)
    quarter = lax.broadcasted_iota(jnp.int32, (8, PAD), 0)
    rows = []
    for k in bins:
        turn = (k * sample + 4 * (quarter - 1)) % UPCHAN
        wave = jnp.cos(turn.astype(jnp.float32) * (2.0 * math.pi / UPCHAN))
        for out in range(2):
            tiles = []
            for lane in range(0, width, PAD):
                for part in range(2):
                    quarters = out - part + 1
                    tiles.append(values[:, lane : lane + PAD] * wave[quarters : quarters + 1, :])
            rows.append(jnp.concatenate(tiles, axis=1))
    table = jnp.concatenate(rows, axis=0)
    high = table.astype(jnp.bfloat16)
    low = (table - high.astype(jnp.float32)).astype(jnp.bfloat16)
    return jnp.concatenate([high, low], axis=0)


def both_halves(table, samples, contract=1):
    total = lax.dot_general(table, samples, (((1,), (contract,)), ((), ())), preferred_element_type=jnp.float32)
    return total[: total.shape[0] // 2] + total[total.shape[0] // 2 :]


def history_kernel(bins_per_coarse, lead_width, volts_ref, tail_ref, pairs_ref):
    width = volts_ref.shape[3]
    values = windows(8, PAD, PAD - lead_width)
    at = 0
    for coarse, bins in enumerate(bins_per_coarse):
        table = group_table(range(bins), values, PAD - lead_width)
        samples = jnp.concatenate(parts_of(volts_ref, pairs_ref, coarse, width - PAD, 0), axis=1)
        total = both_halves(table, samples).reshape(bins, 2, 8, -1)[:, :, :4, :]
        tail_ref[at : at + bins * 8, :] = total.reshape(bins * 8, -1)
        at += bins * 8


def parts_of(samples_ref, pairs_ref, coarse, lane, place=None):
    slots = samples_ref.shape[0]
    pairs = samples_ref[:, coarse, :, lane : lane + PAD].reshape(2 * slots, PAD)
    place = lane * 2 * slots // PAD if place is None else place
    pairs_ref[place : place + 2 * slots, :] = pairs.astype(jnp.float32)
    return [pairs_ref[pl.ds(place + part, slots, stride=2), :].astype(jnp.bfloat16) for part in range(2)]


def channel_kernel(plan, lead_width, volts_ref, *refs):
    spectrum_refs, early_ref, pairs_ref = refs[:-2], refs[-2], refs[-1]
    slots, _, _, width = volts_ref.shape
    frames = width // UPCHAN
    groups = frames // GROUP
    span = PAD + GROUP * UPCHAN
    me = lax.axis_index("chan")
    values = windows(GROUP, span, PAD - lead_width)
    for coarse, members in plan:
        bins = [lax.bitwise_xor(me, distance) if relative else distance for relative, distance, _ in members]
        count = len(bins)
        table = group_table(bins, values, PAD - lead_width)
        samples = [
            jnp.concatenate(parts_of(volts_ref, pairs_ref, coarse, lane), axis=1) for lane in range(0, width, PAD)
        ]
        for group in range(groups):
            total = 0.0
            for lane in range(span // PAD):
                at = group * GROUP * UPCHAN // PAD - 1 + lane
                if at >= 0:
                    columns = slice(2 * lane * PAD, 2 * (lane + 1) * PAD)
                    total = total + both_halves(table[:, columns], samples[at])
            total = total.reshape(count, 2, GROUP, slots)
            if group == 0:
                row = (coarse * UPCHAN) * 8
                early_ref[row : row + count * 8, :] = total[:, :, :4, :].reshape(count * 8, slots)
            for at, (_, _, (out, index)) in enumerate(members):
                for part in range(2):
                    row = part * frames + group * GROUP
                    spectrum_refs[out][index, row : row + GROUP, :] = total[at, part].astype(jnp.bfloat16)


def early_kernel(plan, lead_ref, early_ref, history_ref, *refs):
    head_ref, refs = refs[-1], refs[:-1]
    spectra_in, spectra_out = refs[: len(refs) // 2], refs[len(refs) // 2 :]
    lead_width, slots = lead_ref.shape[2:]
    first = lax.axis_index("tblk") == 0
    me = lax.axis_index("chan")
    head_ref[...] = jnp.zeros_like(head_ref)

    @pl.when(first)
    def _():
        values = windows(8, PAD, PAD - lead_width)
        for coarse, members in plan:
            bins = [lax.bitwise_xor(me, distance) if relative else distance for relative, distance, _ in members]
            table = group_table(bins, values, PAD - lead_width)
            lead = []
            for part in range(2):
                lead += [jnp.zeros((PAD - lead_width, slots), jnp.bfloat16), lead_ref[part, coarse, :, :]]
            head = both_halves(table, jnp.concatenate(lead, axis=0), 0).reshape(len(bins), 2, 8, slots)[:, :, :4, :]
            row = coarse * UPCHAN * 8
            head_ref[row : row + len(bins) * 8, :] = head.reshape(len(bins) * 8, slots)

    for coarse, members in plan:
        bins = [lax.bitwise_xor(me, distance) if relative else distance for relative, distance, _ in members]
        for at, (relative, distance, (out, index)) in enumerate(members):
            frames = spectra_in[out].shape[1] // 2
            bin_at = bins[at] + coarse * UPCHAN
            row = (coarse * UPCHAN + at) * 8
            history = history_ref[pl.ds(pl.multiple_of(bin_at * 8, 8), 8), :]
            total = early_ref[row : row + 8, :] + history + head_ref[row : row + 8, :]
            for part in range(2):
                opening = total if part == 0 else pltpu.roll(total, 4, 0)
                opening = jnp.concatenate([opening, opening], axis=0)
                old = spectra_in[out][index, part * frames : part * frames + GROUP, :].astype(jnp.float32)
                row = lax.broadcasted_iota(jnp.int32, old.shape, 0)
                new = jnp.where(row < 4, opening, old).astype(jnp.bfloat16)
                spectra_out[out][index, part * frames : part * frames + GROUP, :] = new


def choice_kernel(relative, source, slots, slot_ref, choice_ref):
    owner = lax.bitwise_xor(lax.axis_index("chan"), source) if relative else source
    for row in range(0, choice_ref.shape[0], 64):
        rows = min(64, choice_ref.shape[0] - row)
        place = lax.broadcasted_iota(jnp.int32, (rows, slot_ref.shape[1]), 0) + (owner * slots + row)
        choice_ref[row : row + rows, :] = (place == slot_ref[...]).astype(jnp.bfloat16)


def order_kernel(rows, places, fresh, choice_ref, *refs):
    pieces, new_ref = refs[: len(places)], refs[-1]
    put_in_order(rows, places, fresh, choice_ref, pieces, refs[-2], new_ref)


def put_in_order(rows, places, fresh, choice_ref, pieces, old_ref, new_ref):
    frames = rows // 2
    inputs = choice_ref.shape[1]
    stacked = [piece[at * rows : (at + 1) * rows, :] for piece, (_, at) in zip(pieces, places)]
    stacked = jnp.concatenate(stacked, axis=0)
    for column in range(0, inputs, 512):
        total = jnp.dot(stacked, choice_ref[:, column : column + 512], preferred_element_type=jnp.float32)
        total = total.astype(jnp.bfloat16)
        for at, (place, _) in enumerate(places):
            for part in range(2):
                value = total[at * rows + part * frames : at * rows + (part + 1) * frames]
                to = (slice(place * frames, (place + 1) * frames), slice(part * inputs + column, part * inputs + column + 512))
                new_ref[to] = value if fresh else old_ref[to] + value


def after(value, *others):
    return call(
        lambda *refs: None,
        jax.ShapeDtypeStruct(value.shape, value.dtype),
        value,
        *others,
        name="after",
        limit=1,
        spaces=ANY,
        outs=ANY,
        input_output_aliases={0: 0},
    )


def join_kernel(*refs):
    rows = refs[0].shape[0]
    for at, ref in enumerate(refs[:-1]):
        refs[-1][at * rows : (at + 1) * rows, :] = ref[...]


def from_other_core(parts):
    rows, slots = parts[0].shape
    if len(parts) == 1:
        return [(swapped(parts[0], "tblk", 1), 0)]
    joined = call(
        join_kernel, jax.ShapeDtypeStruct((len(parts) * rows, slots), parts[0].dtype), *parts, name="join", limit=4
    )
    other = swapped(joined, "tblk", 1)
    return [(other, at) for at in range(len(parts))]


def gram_kernel(blocks, relative, *refs):
    parts = refs[:-6]
    fine_hbm, gram_hbm, ordered, tile, result, sems = refs[-6:]
    frames = ordered.shape[0] // blocks
    width = tile.shape[0]
    own = 0 if relative else pl.multiple_of(lax.axis_index("tblk") * frames, frames)
    copies = [pltpu.make_async_copy(parts[0].at[pl.ds(own, frames), :], fine_hbm, sems.at[0])]
    copies[0].start()
    row = 0
    for part in parts:
        ordered[row : row + part.shape[0], :] = part[...]
        row += part.shape[0]
    chunk = max(PAD, width // 8)
    for at in range(width // chunk):
        rows = slice(at * chunk, (at + 1) * chunk)
        place = pl.multiple_of(lax.axis_index("tblk") * width + at * chunk, chunk)
        tile[rows, :] = ordered[:, pl.ds(place, chunk)].T
        gram = jnp.dot(tile[rows, :], ordered[...], preferred_element_type=jnp.float32)
        result[rows, :] = (gram * (1.0 / ordered.shape[0])).astype(jnp.bfloat16)
        copy = pltpu.make_async_copy(
            result.at[pl.ds(at * chunk, chunk), :], gram_hbm.at[pl.ds(at * chunk, chunk), :], sems.at[at + 1]
        )
        copy.start()
        copies.append(copy)
    for copy in copies:
        copy.wait()


def call(kernel, shapes, *operands, name, limit, spaces=VMEM, outs=VMEM, flops=0, moved=0, **options):
    spaces = spaces if isinstance(spaces, list) else [spaces] * len(operands)
    several = isinstance(shapes, list)
    return pl.pallas_call(
        kernel,
        in_specs=spaces,
        out_specs=[outs] * len(shapes) if several else outs,
        out_shape=shapes,
        compiler_params=pltpu.CompilerParams(vmem_limit_bytes=limit * MIB),
        name=name,
        cost_estimate=pl.CostEstimate(flops=flops, bytes_accessed=moved, transcendentals=0),
        **options,
    )(*operands)


def local(coarse_volts, lead_in, slot_of_input):
    slots, _, coarse, width = coarse_volts.shape
    lead_width = lead_in.shape[3]
    chans, blocks = lax.axis_size("chan"), lax.axis_size("tblk")
    frames = width // UPCHAN
    inputs = slot_of_input.shape[0]
    relative = coarse == 1 and chans == 4 and blocks == 4
    volts = coarse_volts.transpose(0, 2, 1, 3)
    lead = lead_in.transpose(1, 2, 3, 0)
    order = slot_of_input.reshape(1, inputs)

    per_coarse = [max(0, min(UPCHAN, chans - c * UPCHAN)) for c in range(coarse)]
    shape = jax.ShapeDtypeStruct

    opening = call(
        functools.partial(history_kernel, per_coarse, lead_width),
        shape((chans * 8, slots), jnp.float32),
        volts,
        name="history",
        moved=2 * MIB,
        limit=4,
        scratch_shapes=[pltpu.VMEM((2 * slots, PAD), jnp.float32)],
    )
    history = shifted(opening, "tblk", 1)

    if relative:
        plan = [(0, [(True, distance, (distance, 0)) for distance in range(chans)])]
        shapes = [shape((1, 2 * frames, slots), jnp.bfloat16)] * chans
    else:
        plan = [
            (c, [(False, k, (0, c * UPCHAN + k)) for k in range(count)]) for c, count in enumerate(per_coarse) if count
        ]
        shapes = [shape((chans, 2 * frames, slots), jnp.bfloat16)]
    *spectra, early = call(
        functools.partial(channel_kernel, plan, lead_width),
        shapes + [shape((chans * 8, slots), jnp.float32)],
        volts,
        name="channelize",
        moved=6 * MIB,
        limit=14,
        scratch_shapes=[pltpu.VMEM((2 * slots * width // PAD, PAD), jnp.float32)],
    )
    spectra = call(
        functools.partial(early_kernel, plan),
        shapes,
        lead,
        early,
        history,
        *spectra,
        name="early",
        limit=2,
        scratch_shapes=[pltpu.VMEM((chans * 8, slots), jnp.float32)],
        input_output_aliases={3 + at: at for at in range(len(shapes))},
    )

    sources = range(chans) if relative else [0]
    wide = slots if relative else inputs
    choices = [
        call(
            functools.partial(choice_kernel, relative, source, wide),
            shape((wide, inputs), jnp.bfloat16),
            order,
            name="choice",
            moved=0,
            limit=2 if relative else 10,
        )
        for source in sources
    ]
    mine = blocks // 2 if relative else blocks
    ordered_shape = shape((mine * frames, 2 * inputs), jnp.bfloat16)

    def put(source, given, ordered):
        given = [(to, *piece) for to, piece in given]
        old = [] if ordered is None else [ordered]
        return call(
            functools.partial(order_kernel, 2 * frames, [(to, at) for to, _, at in given], ordered is None),
            ordered_shape,
            choices[source],
            *[array for _, array, _ in given],
            *old,
            name="order",
            flops=4 * len(given) * frames * wide * inputs,
            limit=6 if relative else 24,
            input_output_aliases={1 + len(given): 0} if old else {},
        )

    if relative:
        spectra = [s[0] for s in spectra]
        own, one = spectra[0], spectra[1]
        z2, z3 = swapped(spectra[2], "chan", 2), swapped(spectra[3], "chan", 3)
        z1 = swapped(one, "chan", 1)
        x1 = lax.ppermute(
            one,
            ("chan", "tblk"),
            [(c * blocks + b, (c ^ 1) * blocks + (b ^ 2)) for c in range(chans) for b in range(blocks)],
        )
        x0 = swapped(own, "tblk", 2)
        x3 = swapped(z3, "tblk", 2)
        x2 = swapped(z2, "tblk", 2)
        ordered = put(1, [(0, (z1, 0)), (1, (x1, 0))], None)
        ordered = put(0, [(0, (own, 0)), (1, (x0, 0))], ordered)
        ordered = put(2, [(0, (z2, 0)), (1, (x2, 0))], ordered)
        ordered = put(3, [(0, (z3, 0)), (1, (x3, 0))], ordered)
        halves = [ordered, swapped(ordered, "tblk", 1)]
    else:
        owned = lax.all_to_all(spectra[0], "chan", split_axis=0, concat_axis=2, tiled=True)[0]
        all_time = lax.all_gather(owned, "tblk", axis=0)
        halves = [put(0, [(b, (all_time[b], 0)) for b in range(blocks)], None)]

    tile_rows = 2 * inputs // blocks
    fine, gram = call(
        functools.partial(gram_kernel, blocks, relative),
        [shape((frames, 2 * inputs), jnp.bfloat16), shape((tile_rows, 2 * inputs), jnp.bfloat16)],
        *halves,
        name="gram",
        moved=12 * MIB,
        limit=20 if relative else 40,
        outs=HBM,
        scratch_shapes=[
            pltpu.VMEM((blocks * frames, 2 * inputs), jnp.bfloat16),
            pltpu.VMEM((tile_rows, blocks * frames), jnp.bfloat16),
            pltpu.VMEM((tile_rows, 2 * inputs), jnp.bfloat16),
            pltpu.SemaphoreType.DMA((9,)),
        ],
    )
    return fine[None], gram[None]


def solution(mesh):
    placed = (P("chan", None, "grp", "tblk"), P("chan", None, "grp", None), P())
    return jax.shard_map(
        local,
        mesh=mesh,
        in_specs=placed,
        out_specs=(P(("grp", "chan"), "tblk", None), P(("grp", "chan"), "tblk", None)),
        check_vma=False,
    )
```
